512 devices in a mesh: aux: 16 (over x, y), orb: 32 (over z, core).
Axes of the slice: x: 4, y: 4, z: 16, core: 2. Of those that a mesh axis runs over, the one named last changes fastest.
Arguments:
- tensor: bfloat16 [96, 64, 64, 2048], P('orb', None, None, 'aux'), may hold values from -6 to 6
- nu_index: int32 [32, 3], P('orb'), may hold values from 0 to 31, as said below
- density: bfloat16 [2048, 256], P(('aux', 'orb')), may hold values from -0.4375 to 0.4375
- density_pattern: int32 [32, 4], replicated, may hold values 0 or 1
- blockmap: int32 [32], replicated, may hold values from 0 to 31, each once
- virtual: bfloat16 [2048, 512], P(('aux', 'orb')), may hold values from -0.125 to 0.125
Outputs:
- three_index: bfloat16 [512, 256, 2048], P(None, 'orb', 'aux')
The draws below stay inside these ranges and needn't reach their ends.
Inputs may be any that keep to these rules, and one draw needn't show every extreme that they name: `nu_index`: row r holds 3 different nu blocks, one of them r itself. `blockmap`: each mu block is held by exactly one index of orb.
All inputs are finite; a program needn't handle non-finite values.
Results may differ from the reference program's by a relative error of at most 0.0049.
Values may be sent and summed in bfloat16 or wider, within the bound.
A program may use at most 64 MiB of HBM per device.

```python
import jax
import jax.numpy as jnp
from jax import lax

BLK = 64
SLOTS = 3
LAM_BLOCKS = 4
MU = 2048
LAM = 256
SIG = 512
PAUX = 2048
N_ORB = 32


def draw_nu_index(key, part):
    key = jax.random.fold_in(key, 7)
    row_keys = jax.random.split(key, N_ORB)

    def offsets_for(row_key):
        return jax.random.permutation(row_key, N_ORB - 1)[:SLOTS - 1].astype(jnp.int32) + 1
    offsets = jax.vmap(offsets_for)(row_keys)
    offsets = jnp.concatenate([jnp.zeros((N_ORB, 1), jnp.int32), offsets], 1)
    row_ids = jnp.arange(N_ORB, dtype=jnp.int32)[:, None]
    return (row_ids + offsets) % N_ORB


def with_ends(entries, key, smallest, high):
    longest = entries.shape.index(max(entries.shape))
    spots = []
    for shift in (0, 1):
        where = [jax.random.randint(jax.random.fold_in(key, axis), (), 0, length) for axis, length in enumerate(entries.shape)]
        where[longest] = (where[longest] + shift) % entries.shape[longest]
        spots.append(tuple(where))
    return entries.at[spots[0]].set(smallest).at[spots[1]].set(high)


def levels(own_key, shape, pieces, least, top_value):
    level = 1.0
    for dim, shards_of in pieces:
        heights = jax.random.uniform(jax.random.fold_in(jax.random.fold_in(own_key, 6), dim), (shards_of,), jnp.float32, least / len(pieces), top_value / len(pieces))
        level = level * jnp.repeat(jnp.exp(heights), shape[dim] // shards_of).reshape((-1,) + (1,) * (len(shape) - 1 - dim))
    return level


def gaussian(own_key, extent, scale, reach, shards=(), kind=jnp.bfloat16):
    values = scale * jax.random.normal(own_key, extent, jnp.float32)
    if shards:
        values = values * levels(own_key, extent, shards, -0.22, 0.18)
    return jnp.clip(values, -reach, reach).astype(kind)


def setup_inputs(seed: int = 0) -> dict:
    keys = jax.random.split(jax.random.key(seed), 7)
    tensor = gaussian(keys[0], (N_ORB * SLOTS, BLK, BLK, PAUX), 1.0, 6.0, ((0, 32), (3, 16)))
    nu_index = draw_nu_index(jax.random.fold_in(keys[6], 71), 0)
    density = gaussian(keys[2], (MU, LAM), (SLOTS * BLK) ** -0.5, 0.4375, ((0, 512),))
    density_pattern = with_ends((jax.random.randint(keys[3], (N_ORB, LAM_BLOCKS), 0, 4) < 3).astype(jnp.int32), jax.random.fold_in(keys[3], 1), 0, 1)
    blockmap = jax.random.permutation(keys[4], N_ORB).astype(jnp.int32)
    virtual = gaussian(keys[5], (MU, SIG), MU ** -0.5, 0.125, ((0, 512),))
    return dict(tensor=tensor, nu_index=nu_index, density=density, density_pattern=density_pattern, blockmap=blockmap, virtual=virtual)


def reference(tensor, nu_index, density, density_pattern, blockmap, virtual):
    kept_mask = jnp.repeat(jnp.repeat(density_pattern, BLK, axis=0), BLK, axis=1) > 0
    masked = jnp.where(kept_mask, density, jnp.zeros_like(density))

    def one_owner(accumulated, owner_index):
        row_blocks = [lax.dynamic_slice_in_dim(masked, (nu_index[owner_index, slot_index] * BLK).astype(jnp.int32), BLK, 0) for slot_index in range(SLOTS)]
        chosen = jnp.concatenate(row_blocks, 0)
        stored = lax.dynamic_slice_in_dim(tensor, (owner_index * SLOTS).astype(jnp.int32), SLOTS, 0)
        flattened = stored.reshape(SLOTS * BLK, BLK * PAUX)
        half_done = lax.dot_general(chosen, flattened, (((0,), (0,)), ((), ())), preferred_element_type=jnp.float32)
        half_done = half_done.astype(jnp.bfloat16).reshape(LAM, BLK, PAUX)
        virtual_rows = lax.dynamic_slice_in_dim(virtual, (blockmap[owner_index] * BLK).astype(jnp.int32), BLK, 0)
        accumulated = accumulated + jnp.einsum('ms,lmp->slp', virtual_rows.astype(jnp.float32), half_done.astype(jnp.float32))
        return accumulated, None

    initial = jnp.zeros((SIG, LAM, PAUX), jnp.float32)
    accumulated, unused = lax.scan(one_owner, initial, jnp.arange(N_ORB, dtype=jnp.int32))
    return accumulated.astype(jnp.bfloat16)
```

```python
import functools

import jax
import jax.numpy as jnp
from jax import lax
from jax.experimental import pallas as pl
from jax.experimental.pallas import tpu as pltpu
from jax.sharding import PartitionSpec as P

MESH = pl.DeviceIdType.MESH
BF16 = jnp.bfloat16
F32 = jnp.float32
BLK = 64
LANES = 128
REACH = 4
CHUNKS = 4
PAIR = 2


def kernel(
    aux_n, chips, nu_ref, pat_ref, bm_ref, dens_ref, virt_ref, t_hbm, out_ref,
    tbuf, big, tt, piece, d_in, d_all, v_all, d_sc, v_sc, d_nat, d_t, v_own, v_far,
    half, far, sib, part, hop,
    t_sem, a_snd, a_rcv, b_snd, b_rcv, c_snd, c_rcv, n_snd, n_rcv, f_snd, f_rcv, p_snd, p_rcv,
):
    aux = lax.axis_index("aux")
    orb = lax.axis_index("orb")
    chip = lax.div(orb, 2)
    core = lax.rem(orb, 2)
    other = 1 - core
    mate = (aux, 2 * chip + other)

    def ring(shift):
        return lax.rem(chip + shift + 2 * chips, chips)

    def remote(src, dst, snd, rcv, to):
        return pltpu.make_async_remote_copy(
            src_ref=src, dst_ref=dst, send_sem=snd, recv_sem=rcv, device_id=to, device_id_type=MESH
        )

    load_t = pltpu.make_async_copy(t_hbm, tbuf, t_sem)
    load_t.start()

    barrier = pltpu.get_barrier_semaphore()

    def greet(to):
        pl.semaphore_signal(barrier, inc=1, device_id=to, device_id_type=MESH)

    @pl.loop(1, chips)
    def _(i):
        greet((aux, 2 * ring(i) + core))

    @pl.loop(1, aux_n)
    def _(i):
        greet((lax.rem(aux + i, aux_n), orb))

    for j in range(1, REACH + 1):
        greet((aux, 2 * ring(j) + other))
        greet((aux, 2 * ring(-j) + other))
    greet(mate)

    dens = dens_ref[...].astype(F32)
    for b in range(2):
        d_in[chip, pl.ds(b, 4, stride=2), :] = dens[:, b * LANES : (b + 1) * LANES]
    virt = virt_ref[...].astype(F32)
    for b in range(4):
        piece[pl.ds(b, 4, stride=4), :] = virt[:, b * LANES : (b + 1) * LANES]
    span = chips // 2
    v_all[core, 2 * aux + lax.div(chip, span), lax.rem(chip, span)] = piece[...].astype(BF16)

    pl.semaphore_wait(barrier, (chips - 1) + (aux_n - 1) + 2 * REACH + 1)

    def d_along(i):
        return remote(d_in.at[chip], d_in.at[chip], a_snd.at[0, i], a_rcv.at[0, i], (aux, 2 * ring(i) + core))

    def v_along(i):
        mine = v_all.at[core, 2 * aux + lax.div(chip, span), lax.rem(chip, span)]
        return remote(mine, mine, a_snd.at[1, i], a_rcv.at[1, i], (aux, 2 * ring(i) + core))

    @pl.loop(1, chips)
    def _(i):
        d_along(i).start()

    @pl.loop(1, chips)
    def _(i):
        v_along(i).start()

    load_t.wait()

    @pl.loop(0, 3 * BLK // 8)
    def _(i):
        rows = tbuf[lax.div(i, 8), pl.ds(lax.rem(i, 8) * 8, 8)]
        big[pl.ds(pl.multiple_of(i * 512, 512), 512), :] = rows.astype(F32).reshape(512, LANES)

    @pl.loop(0, BLK)
    def _(m):
        tt[m] = big[pl.ds(m, 3 * BLK, stride=BLK), :].astype(BF16)

    @pl.loop(1, chips)
    def _(i):
        d_along(i).wait_recv()

    d_all[core, pl.ds(2 * aux, 2)] = d_in[...].reshape(2, BLK, LANES).astype(BF16)

    def d_plane(i):
        mine = d_all.at[core, pl.ds(2 * aux, 2)]
        return remote(mine, mine, b_snd.at[0, i], b_rcv.at[0, i], (lax.rem(aux + i, aux_n), orb))

    def v_plane(i):
        mine = v_all.at[core, pl.ds(2 * aux, 2)]
        return remote(mine, mine, b_snd.at[1, i], b_rcv.at[1, i], (lax.rem(aux + i, aux_n), orb))

    @pl.loop(1, aux_n)
    def _(i):
        d_plane(i).start()

    @pl.loop(1, chips)
    def _(i):
        v_along(i).wait_recv()

    @pl.loop(1, aux_n)
    def _(i):
        d_plane(i).wait_recv()

    d_mate = remote(d_all.at[core], d_all.at[core], c_snd.at[0], c_rcv.at[0], mate)
    v_mate = remote(v_all.at[core], v_all.at[core], c_snd.at[1], c_rcv.at[1], mate)
    d_mate.start()

    @pl.loop(1, aux_n)
    def _(i):
        v_plane(i).start()

    d_mate.wait_recv()

    lane = lax.broadcasted_iota(jnp.int32, (BLK, LANES), 1)
    d_nat[3 * BLK :, :] = jnp.zeros((BLK, 2 * LANES), F32)
    for s in range(3):
        nu = nu_ref[0, s]
        for c in range(2):
            d_sc[:, c] = d_all[c, nu].astype(F32).reshape(8, 8, LANES)
        flat = d_sc.reshape(2 * BLK, LANES)
        for b in range(2):
            rows = flat[pl.ds(b, BLK, stride=2), :]
            keep = jnp.where(lane < BLK, pat_ref[nu, 2 * b], pat_ref[nu, 2 * b + 1]) > 0
            d_nat[s * BLK : (s + 1) * BLK, b * LANES : (b + 1) * LANES] = jnp.where(keep, rows, 0.0)
    d_t[...] = d_nat[...].T.astype(BF16)

    @pl.loop(0, BLK // 2)
    def _(i):
        two = jnp.concatenate([tt[2 * i], tt[2 * i + 1]], axis=1)
        prod = jnp.dot(d_t[:, : 3 * BLK], two, preferred_element_type=F32)
        big[pl.ds(2 * i, 256, stride=BLK), :] = prod[:, :LANES]
        big[pl.ds(2 * i + 1, 256, stride=BLK), :] = prod[:, LANES:]

    def round_half(o):
        rows = big[pl.ds(pl.multiple_of(o * 512, 512), 512), :]
        half[o] = rows.astype(BF16).reshape(8, BLK, LANES)

    def far_copy(way, j, c, q, slot, where):
        sign = 1 - 2 * way
        o = 2 * ring(sign * (REACH + j)) + c
        cols = pl.ds(q * PAIR, PAIR)
        return remote(
            half.at[o, cols], far.at[way, slot, cols], f_snd.at[way, where, q], f_rcv.at[way, slot, q],
            (aux, 2 * ring(sign * j) + c),
        )

    def far_all(q):
        copies = []
        for c in range(2):
            copies.append(far_copy(core, REACH, c, q, 2 * REACH - 2, 2 * REACH - 2 + c))
            for j in range(REACH - 1, 0, -1):
                for way in range(2):
                    copies.append(far_copy(way, j, c, q, 2 * (j - 1) + core, 2 * (j - 1) + c))
        return copies

    @pl.loop(REACH + 1, chips - REACH)
    def _(e):
        for c in range(2):
            round_half(2 * ring(e) + c)

    @pl.loop(0, CHUNKS)
    def _(q):
        for copy in far_all(q):
            copy.start()

    def near_copy(e):
        return remote(half.at[2 * ring(e - REACH) + other], sib.at[e], n_snd.at[e], n_rcv.at[e], mate)

    @pl.loop(0, 2 * REACH + 1)
    def _(e):
        for c in range(2):
            round_half(2 * ring(e - REACH) + c)
        near_copy(e).start()

    @pl.loop(1, aux_n)
    def _(i):
        v_plane(i).wait_recv()

    v_mate.start()
    v_mate.wait_recv()

    def turned(first, second, put):
        for n, o in enumerate((first, second)):
            b = bm_ref[o]
            for c in range(2):
                v_sc[n, :, c] = v_all[c, b].astype(F32)
        flat = v_sc.reshape(2 * 4 * BLK, LANES)
        for b in range(4):
            rows = flat[pl.ds(b, 2 * BLK, stride=4), :]
            put(slice(b * LANES, (b + 1) * LANES), rows.T.astype(BF16))

    def put_own(rows, val):
        v_own[rows, :] = val
        for way in range(2):
            v_far[way, rows, 0:LANES] = val

    turned(orb, 2 * chip + other, put_own)
    for way in range(2):
        for j in range(1, REACH + 1):
            z = ring(-j if way == 0 else j)

            def put_far(rows, val):
                v_far[way, rows, j * LANES : (j + 1) * LANES] = val

            if j < REACH:
                turned(2 * z, 2 * z + 1, put_far)
            else:
                turned(2 * z + way, 2 * z + way, put_far)

    def own_blocks(e, q, k):
        lam = q * PAIR + k
        return [half[2 * ring(e) + core, lam], sib[e + REACH, lam]]

    def hop_copy(way, k, q):
        sign = 1 - 2 * way
        src = part.at[way, q] if k == 0 else hop.at[way, k - 1, q]
        return remote(src, hop.at[way, k, q], p_snd.at[way, k, q], p_rcv.at[way, k, q], (aux, 2 * ring(sign) + core))

    @pl.loop(0, 2 * REACH + 1)
    def _(e):
        near_copy(e).wait_recv()

    depth = (2 * REACH + 1) * BLK

    @pl.loop(0, CHUNKS)
    def _(q):
        for way in range(2):
            for slot in range(2 * REACH - 1):
                far_copy(way, 1, 0, q, slot, 0).wait_recv()
            cols = []
            for k in range(PAIR):
                blocks = own_blocks((1 - 2 * way) * REACH, q, k)
                blocks += [far[way, slot, q * PAIR + k] for slot in range(2 * REACH - 1)]
                cols.append(jnp.concatenate(blocks, axis=0))
            x = jnp.concatenate(cols, axis=1)
            part[way, q] = jnp.dot(v_far[way, :, :depth], x, preferred_element_type=F32).astype(BF16)
            hop_copy(way, 0, q).start()

    def own_term(e, q):
        x = jnp.concatenate([jnp.concatenate(own_blocks(e, q, k), axis=0) for k in range(PAIR)], axis=1)
        return jnp.dot(v_own[...], x, preferred_element_type=F32)

    for k in range(REACH - 1):
        @pl.loop(0, CHUNKS)
        def _(q):
            for way in range(2):
                hop_copy(way, k, q).wait_recv()
                e = (1 - 2 * way) * (REACH - 1 - k)
                total = own_term(e, q) + hop[way, k, q].astype(F32)
                hop[way, k, q] = total.astype(BF16)
                hop_copy(way, k + 1, q).start()

    @pl.loop(0, CHUNKS)
    def _(q):
        total = own_term(0, q)
        for way in range(2):
            hop_copy(way, REACH - 1, q).wait_recv()
            total += hop[way, REACH - 1, q].astype(F32)
        for k in range(PAIR):
            big[pl.ds(q * PAIR + k, 512, stride=8), :] = total[:, k * LANES : (k + 1) * LANES]

    @pl.loop(0, 16)
    def _(i):
        rows = pl.ds(pl.multiple_of(i * 256, 256), 256)
        out_ref[rows, :] = big[rows, :].astype(BF16)

    @pl.loop(1, chips)
    def _(i):
        d_along(i).wait_send()
        v_along(i).wait_send()

    @pl.loop(1, aux_n)
    def _(i):
        d_plane(i).wait_send()
        v_plane(i).wait_send()

    d_mate.wait_send()
    v_mate.wait_send()

    @pl.loop(0, 2 * REACH + 1)
    def _(e):
        near_copy(e).wait_send()

    @pl.loop(0, CHUNKS)
    def _(q):
        for copy in far_all(q):
            copy.wait_send()
        for way in range(2):
            for k in range(REACH):
                hop_copy(way, k, q).wait_send()


def on_device(tensor, nu_index, density, density_pattern, blockmap, virtual):
    aux_n, orb_n = lax.axis_size("aux"), lax.axis_size("orb")
    chips = orb_n // 2
    dma = pltpu.SemaphoreType.DMA
    vmem = pl.BlockSpec(memory_space=pltpu.VMEM)
    smem = pl.BlockSpec(memory_space=pltpu.SMEM)
    out = pl.pallas_call(
        functools.partial(kernel, aux_n, chips),
        out_shape=jax.ShapeDtypeStruct((512 * 8, LANES), BF16),
        in_specs=[smem, smem, smem, vmem, vmem, pl.BlockSpec(memory_space=pl.ANY)],
        out_specs=vmem,
        scratch_shapes=[
            pltpu.VMEM((3, BLK, BLK, LANES), BF16),
            pltpu.VMEM((256 * BLK, LANES), F32),
            pltpu.VMEM((BLK, 3 * BLK, LANES), BF16),
            pltpu.VMEM((16, LANES), F32),
            pltpu.VMEM((chips, 8, LANES), F32),
            pltpu.VMEM((2, 2 * aux_n, BLK, LANES), BF16),
            pltpu.VMEM((2, 2 * aux_n, chips // 2, 16, LANES), BF16),
            pltpu.VMEM((8, 2, 8, LANES), F32),
            pltpu.VMEM((2, 8, 2, 16, LANES), F32),
            pltpu.VMEM((4 * BLK, 2 * LANES), F32),
            pltpu.VMEM((2 * LANES, 4 * BLK), BF16),
            pltpu.VMEM((512, LANES), BF16),
            pltpu.VMEM((2, 512, (REACH + 1) * LANES), BF16),
            pltpu.VMEM((orb_n, 8, BLK, LANES), BF16),
            pltpu.VMEM((2, 2 * REACH - 1, 8, BLK, LANES), BF16),
            pltpu.VMEM((2 * REACH + 1, 8, BLK, LANES), BF16),
            pltpu.VMEM((2, CHUNKS, 512, PAIR * LANES), BF16),
            pltpu.VMEM((2, REACH, CHUNKS, 512, PAIR * LANES), BF16),
            dma,
            dma((2, chips)), dma((2, chips)),
            dma((2, aux_n)), dma((2, aux_n)),
            dma((2,)), dma((2,)),
            dma((2 * REACH + 1,)), dma((2 * REACH + 1,)),
            dma((2, 2 * REACH, CHUNKS)), dma((2, 2 * REACH, CHUNKS)),
            dma((2, REACH, CHUNKS)), dma((2, REACH, CHUNKS)),
        ],
        compiler_params=pltpu.CompilerParams(
            collective_id=0, has_side_effects=True, vmem_limit_bytes=56 * 2**20
        ),
        cost_estimate=pl.CostEstimate(flops=3 * 10**9, bytes_accessed=5 * 2**20, transcendentals=0),
        name="contract",
    )(nu_index, density_pattern, blockmap, density, virtual, tensor)
    return out.reshape(512, 8, LANES)


def solution(mesh):
    in_specs = (
        P("orb", None, None, "aux"),
        P("orb", None),
        P(("aux", "orb"), None),
        P(),
        P(),
        P(("aux", "orb"), None),
    )
    out_specs = P(None, "orb", "aux")
    return jax.shard_map(
        on_device, mesh=mesh, in_specs=in_specs, out_specs=out_specs, check_vma=False
    )
```

```python
import functools

import jax
import jax.numpy as jnp
from jax import lax
from jax.experimental import pallas as pl
from jax.experimental.pallas import tpu as pltpu
from jax.sharding import PartitionSpec as P

MESH = pl.DeviceIdType.MESH
BF16 = jnp.bfloat16
F32 = jnp.float32
BLK = 64
LANES = 128
REACH = 4
CHUNKS = 4
PAIR = 2


def kernel(
    aux_n, chips, nu_ref, pat_ref, bm_ref, dens_ref, virt_ref, t_hbm, out_ref,
    tbuf, big, tt, piece, d_in, d_all, v_all, d_sc, v_sc, d_nat, d_t, v_own, v_far,
    perm, mid, x_far, x_near, far, sib, part, hop,
    t_sem, a_snd, a_rcv, b_snd, b_rcv, c_snd, c_rcv, n_snd, n_rcv, f_snd, f_rcv, p_snd, p_rcv,
):
    aux = lax.axis_index("aux")
    orb = lax.axis_index("orb")
    chip = lax.div(orb, 2)
    core = lax.rem(orb, 2)
    other = 1 - core
    mate = (aux, 2 * chip + other)

    def ring(shift):
        return lax.rem(chip + shift + 2 * chips, chips)

    def remote(src, dst, snd, rcv, to):
        return pltpu.make_async_remote_copy(
            src_ref=src, dst_ref=dst, send_sem=snd, recv_sem=rcv, device_id=to, device_id_type=MESH
        )

    load_t = pltpu.make_async_copy(t_hbm, tbuf, t_sem)
    load_t.start()

    barrier = pltpu.get_barrier_semaphore()

    def greet(to):
        pl.semaphore_signal(barrier, inc=1, device_id=to, device_id_type=MESH)

    @pl.loop(1, chips)
    def _(i):
        greet((aux, 2 * ring(i) + core))

    @pl.loop(1, aux_n)
    def _(i):
        greet((lax.rem(aux + i, aux_n), orb))

    for j in range(1, REACH + 1):
        greet((aux, 2 * ring(j) + other))
        greet((aux, 2 * ring(-j) + other))
    greet(mate)

    row = lax.broadcasted_iota(jnp.int32, (256, 256), 0)
    col = lax.broadcasted_iota(jnp.int32, (256, 256), 1)
    perm[...] = jnp.where(row == lax.rem(col, 16) * 16 + lax.div(col, 16), 1.0, 0.0).astype(BF16)

    dens = dens_ref[...].astype(F32)
    for b in range(2):
        d_in[chip, pl.ds(b, 4, stride=2), :] = dens[:, b * LANES : (b + 1) * LANES]
    virt = virt_ref[...].astype(F32)
    for b in range(4):
        piece[pl.ds(b, 4, stride=4), :] = virt[:, b * LANES : (b + 1) * LANES]
    span = chips // 2
    v_all[core, 2 * aux + lax.div(chip, span), lax.rem(chip, span)] = piece[...].astype(BF16)

    pl.semaphore_wait(barrier, (chips - 1) + (aux_n - 1) + 2 * REACH + 1)

    def d_along(i):
        return remote(d_in.at[chip], d_in.at[chip], a_snd.at[0, i], a_rcv.at[0, i], (aux, 2 * ring(i) + core))

    def v_along(i):
        mine = v_all.at[core, 2 * aux + lax.div(chip, span), lax.rem(chip, span)]
        return remote(mine, mine, a_snd.at[1, i], a_rcv.at[1, i], (aux, 2 * ring(i) + core))

    @pl.loop(0, chips - 1)
    def _(i):
        step = lax.div(i + 1, 2)
        d_along(chips // 2 + step * (1 - 2 * lax.rem(i, 2))).start()

    load_t.wait()

    @pl.loop(0, 3 * BLK // 8)
    def _(i):
        rows = tbuf[lax.div(i, 8), pl.ds(lax.rem(i, 8) * 8, 8)]
        big[pl.ds(pl.multiple_of(i * 512, 512), 512), :] = rows.astype(F32).reshape(512, LANES)

    @pl.loop(0, BLK)
    def _(m):
        tt[m] = big[pl.ds(m, 3 * BLK, stride=BLK), :].astype(BF16)

    @pl.loop(1, chips)
    def _(i):
        d_along(i).wait_recv()

    d_all[core, pl.ds(2 * aux, 2)] = d_in[...].reshape(2, BLK, LANES).astype(BF16)

    def d_plane(i):
        mine = d_all.at[core, pl.ds(2 * aux, 2)]
        return remote(mine, mine, b_snd.at[0, i], b_rcv.at[0, i], (lax.rem(aux + i, aux_n), orb))

    def v_plane(i):
        mine = v_all.at[core, pl.ds(2 * aux, 2)]
        return remote(mine, mine, b_snd.at[1, i], b_rcv.at[1, i], (lax.rem(aux + i, aux_n), orb))

    @pl.loop(1, aux_n)
    def _(i):
        d_plane(i).start()

    @pl.loop(1, chips)
    def _(i):
        v_along(i).start()

    @pl.loop(1, aux_n)
    def _(i):
        d_plane(i).wait_recv()

    d_mate = remote(d_all.at[core], d_all.at[core], c_snd.at[0], c_rcv.at[0], mate)
    v_mate = remote(v_all.at[core], v_all.at[core], c_snd.at[1], c_rcv.at[1], mate)
    d_mate.start()

    @pl.loop(1, chips)
    def _(i):
        v_along(i).wait_recv()

    @pl.loop(1, aux_n)
    def _(i):
        v_plane(i).start()

    d_mate.wait_recv()

    lane = lax.broadcasted_iota(jnp.int32, (BLK, LANES), 1)
    d_nat[3 * BLK :, :] = jnp.zeros((BLK, 2 * LANES), F32)
    for s in range(3):
        nu = nu_ref[0, s]
        for c in range(2):
            d_sc[:, c] = d_all[c, nu].astype(F32).reshape(8, 8, LANES)
        flat = d_sc.reshape(2 * BLK, LANES)
        for b in range(2):
            rows = flat[pl.ds(b, BLK, stride=2), :]
            keep = jnp.where(lane < BLK, pat_ref[2 * b, nu], pat_ref[2 * b + 1, nu]) > 0
            d_nat[s * BLK : (s + 1) * BLK, b * LANES : (b + 1) * LANES] = jnp.where(keep, rows, 0.0)
    turned_d = d_nat[...].T.astype(BF16)
    for b in range(2):
        d_t[b * 4 * BLK : (b + 1) * 4 * BLK, :] = turned_d

    n_far, n_near = chips - 2 * REACH - 1, 2 * REACH + 1

    def halves(first, count):
        low = pl.multiple_of(lax.rem(16 * (chip + first), 16 * chips), 16)
        lhs = d_t[pl.ds(low, 16 * count), : 3 * BLK]

        @pl.loop(0, BLK // 2, unroll=4)
        def _(i):
            two = jnp.concatenate([tt[2 * i], tt[2 * i + 1]], axis=1)
            prod = jnp.dot(lhs, two, preferred_element_type=F32).astype(BF16)
            mid[2 * i, : 16 * count, :] = prod[:, :LANES]
            mid[2 * i + 1, : 16 * count, :] = prod[:, LANES:]

    def swap(g, put):
        cols = pl.ds(pl.multiple_of(g * 16, 16), 16)
        for i in range(0, 4, 2):
            two = [mid[16 * n : 16 * n + 16, cols, :].reshape(256, LANES) for n in (i, i + 1)]
            prod = jnp.dot(perm[...], jnp.concatenate(two, axis=1), preferred_element_type=F32).astype(BF16)
            for n in range(2):
                rows = slice(16 * (i + n), 16 * (i + n) + 16)
                put(rows, prod[:, n * LANES : (n + 1) * LANES].reshape(2, 8, 16, LANES))

    def far_copy(way, j, c, q, slot, where):
        sign = 1 - 2 * way
        spot = sign * (REACH + j) + chips * way - REACH - 1
        cols = pl.ds(q * PAIR, PAIR)
        return remote(
            x_far.at[spot, c, cols], far.at[way, slot, cols], f_snd.at[way, where, q], f_rcv.at[way, slot, q],
            (aux, 2 * ring(sign * j) + c),
        )

    def far_all(q):
        copies = []
        for c in range(2):
            copies.append(far_copy(core, REACH, c, q, 2 * REACH - 2, 2 * REACH - 2 + c))
            for j in range(REACH - 1, 0, -1):
                for way in range(2):
                    copies.append(far_copy(way, j, c, q, 2 * (j - 1) + core, 2 * (j - 1) + c))
        return copies

    halves(REACH + 1, n_far)

    @pl.loop(0, n_far)
    def _(g):
        def put(rows, val):
            x_far[g, :, :, rows, :] = val

        swap(g, put)

    @pl.loop(0, CHUNKS)
    def _(q):
        for copy in far_all(q):
            copy.start()

    def near_copy(e):
        return remote(x_near.at[e, other], sib.at[e], n_snd.at[e], n_rcv.at[e], mate)

    halves(chips - REACH, n_near)

    @pl.loop(0, n_near)
    def _(e):
        def put(rows, val):
            x_near[e, :, :, rows, :] = val

        swap(e, put)
        near_copy(e).start()

    @pl.loop(1, aux_n)
    def _(i):
        v_plane(i).wait_recv()

    v_mate.start()
    v_mate.wait_recv()

    def turned(first, second, put):
        for n, o in enumerate((first, second)):
            b = bm_ref[o]
            for c in range(2):
                v_sc[n, :, c] = v_all[c, b].astype(F32)
        flat = v_sc.reshape(2 * 4 * BLK, LANES)
        for b in range(4):
            rows = flat[pl.ds(b, 2 * BLK, stride=4), :]
            put(slice(b * LANES, (b + 1) * LANES), rows.T.astype(BF16))

    def put_own(rows, val):
        v_own[rows, :] = val
        for way in range(2):
            v_far[way, rows, 0:LANES] = val

    turned(orb, 2 * chip + other, put_own)
    for way in range(2):
        for j in range(1, REACH + 1):
            z = ring(-j if way == 0 else j)

            def put_far(rows, val):
                v_far[way, rows, j * LANES : (j + 1) * LANES] = val

            if j < REACH:
                turned(2 * z, 2 * z + 1, put_far)
            else:
                turned(2 * z + way, 2 * z + way, put_far)

    def own_blocks(e, q, k):
        lam = q * PAIR + k
        return [x_near[e + REACH, core, lam], sib[e + REACH, lam]]

    def hop_copy(way, k, q):
        sign = 1 - 2 * way
        src = part.at[way, q] if k == 0 else hop.at[way, k - 1, q]
        return remote(src, hop.at[way, k, q], p_snd.at[way, k, q], p_rcv.at[way, k, q], (aux, 2 * ring(sign) + core))

    @pl.loop(0, 2 * REACH + 1)
    def _(e):
        near_copy(e).wait_recv()

    depth = (2 * REACH + 1) * BLK

    @pl.loop(0, CHUNKS)
    def _(q):
        for way in range(2):
            for slot in range(2 * REACH - 1):
                far_copy(way, 1, 0, q, slot, 0).wait_recv()
            cols = []
            for k in range(PAIR):
                blocks = own_blocks((1 - 2 * way) * REACH, q, k)
                blocks += [far[way, slot, q * PAIR + k] for slot in range(2 * REACH - 1)]
                cols.append(jnp.concatenate(blocks, axis=0))
            x = jnp.concatenate(cols, axis=1)
            part[way, q] = jnp.dot(v_far[way, :, :depth], x, preferred_element_type=F32).astype(BF16)
            hop_copy(way, 0, q).start()

    def own_term(e, q):
        x = jnp.concatenate([jnp.concatenate(own_blocks(e, q, k), axis=0) for k in range(PAIR)], axis=1)
        return jnp.dot(v_own[...], x, preferred_element_type=F32)

    for k in range(REACH - 1):
        @pl.loop(0, CHUNKS)
        def _(q):
            for way in range(2):
                hop_copy(way, k, q).wait_recv()
                e = (1 - 2 * way) * (REACH - 1 - k)
                total = own_term(e, q) + hop[way, k, q].astype(F32)
                hop[way, k, q] = total.astype(BF16)
                hop_copy(way, k + 1, q).start()

    @pl.loop(0, CHUNKS)
    def _(q):
        total = own_term(0, q)
        for way in range(2):
            hop_copy(way, REACH - 1, q).wait_recv()
            total += hop[way, REACH - 1, q].astype(F32)
        for k in range(PAIR):
            big[pl.ds(q * PAIR + k, 512, stride=8), :] = total[:, k * LANES : (k + 1) * LANES]

    @pl.loop(0, 16)
    def _(i):
        rows = pl.ds(pl.multiple_of(i * 256, 256), 256)
        out_ref[rows, :] = big[rows, :].astype(BF16)

    @pl.loop(1, chips)
    def _(i):
        d_along(i).wait_send()
        v_along(i).wait_send()

    @pl.loop(1, aux_n)
    def _(i):
        d_plane(i).wait_send()
        v_plane(i).wait_send()

    d_mate.wait_send()
    v_mate.wait_send()

    @pl.loop(0, 2 * REACH + 1)
    def _(e):
        near_copy(e).wait_send()

    @pl.loop(0, CHUNKS)
    def _(q):
        for copy in far_all(q):
            copy.wait_send()
        for way in range(2):
            for k in range(REACH):
                hop_copy(way, k, q).wait_send()


def on_device(tensor, nu_index, density, density_pattern, blockmap, virtual):
    aux_n, orb_n = lax.axis_size("aux"), lax.axis_size("orb")
    chips = orb_n // 2
    dma = pltpu.SemaphoreType.DMA
    vmem = pl.BlockSpec(memory_space=pltpu.VMEM)
    smem = pl.BlockSpec(memory_space=pltpu.SMEM)
    out = pl.pallas_call(
        functools.partial(kernel, aux_n, chips),
        out_shape=jax.ShapeDtypeStruct((512 * 8, LANES), BF16),
        in_specs=[smem, smem, smem, vmem, vmem, pl.BlockSpec(memory_space=pl.ANY)],
        out_specs=vmem,
        scratch_shapes=[
            pltpu.VMEM((3, BLK, BLK, LANES), BF16),
            pltpu.VMEM((256 * BLK, LANES), F32),
            pltpu.VMEM((BLK, 3 * BLK, LANES), BF16),
            pltpu.VMEM((16, LANES), F32),
            pltpu.VMEM((chips, 8, LANES), F32),
            pltpu.VMEM((2, 2 * aux_n, BLK, LANES), BF16),
            pltpu.VMEM((2, 2 * aux_n, chips // 2, 16, LANES), BF16),
            pltpu.VMEM((8, 2, 8, LANES), F32),
            pltpu.VMEM((2, 8, 2, 16, LANES), F32),
            pltpu.VMEM((4 * BLK, 2 * LANES), F32),
            pltpu.VMEM((4 * LANES, 4 * BLK), BF16),
            pltpu.VMEM((512, LANES), BF16),
            pltpu.VMEM((2, 512, (REACH + 1) * LANES), BF16),
            pltpu.VMEM((256, 256), BF16),
            pltpu.VMEM((BLK, 16 * (2 * REACH + 1), LANES), BF16),
            pltpu.VMEM((chips - 2 * REACH - 1, 2, 8, BLK, LANES), BF16),
            pltpu.VMEM((2 * REACH + 1, 2, 8, BLK, LANES), BF16),
            pltpu.VMEM((2, 2 * REACH - 1, 8, BLK, LANES), BF16),
            pltpu.VMEM((2 * REACH + 1, 8, BLK, LANES), BF16),
            pltpu.VMEM((2, CHUNKS, 512, PAIR * LANES), BF16),
            pltpu.VMEM((2, REACH, CHUNKS, 512, PAIR * LANES), BF16),
            dma,
            dma((2, chips)), dma((2, chips)),
            dma((2, aux_n)), dma((2, aux_n)),
            dma((2,)), dma((2,)),
            dma((2 * REACH + 1,)), dma((2 * REACH + 1,)),
            dma((2, 2 * REACH, CHUNKS)), dma((2, 2 * REACH, CHUNKS)),
            dma((2, REACH, CHUNKS)), dma((2, REACH, CHUNKS)),
        ],
        compiler_params=pltpu.CompilerParams(
            collective_id=0, has_side_effects=True, vmem_limit_bytes=56 * 2**20
        ),
        cost_estimate=pl.CostEstimate(flops=3 * 10**9, bytes_accessed=5 * 2**20, transcendentals=0),
        name="contract",
    )(nu_index, density_pattern.T, blockmap, density, virtual, tensor)
    return out.reshape(512, 8, LANES)


def solution(mesh):
    in_specs = (
        P("orb", None, None, "aux"),
        P("orb", None),
        P(("aux", "orb"), None),
        P(),
        P(),
        P(("aux", "orb"), None),
    )
    out_specs = P(None, "orb", "aux")
    return jax.shard_map(
        on_device, mesh=mesh, in_specs=in_specs, out_specs=out_specs, check_vma=False
    )
```

```python
import functools

import jax
import jax.numpy as jnp
from jax import lax
from jax.experimental import pallas as pl
from jax.experimental.pallas import tpu as pltpu
from jax.sharding import PartitionSpec as P

MESH = pl.DeviceIdType.MESH
BF16 = jnp.bfloat16
F32 = jnp.float32
BLK = 64
LANES = 128
REACH = 4
CHUNKS = 4
PAIR = 2


def kernel(
    aux_n, chips, nu_ref, pat_ref, bm_ref, dens_ref, virt_ref, t_hbm, out_ref,
    tbuf, big, tt, piece, nu_out, nu_in, nu_mate, pair_of, d_out, d_in, d_rot, d_first, d_second, d_t, v_all, v_sc, v_own, v_far,
    perm, mid, x, far, far_end, part, hop,
    t_sem, n_sem, a_snd, a_rcv, e_snd, e_rcv, b_snd, b_rcv, w_snd, w_rcv, m_snd, m_rcv, f_snd, f_rcv, p_snd, p_rcv,
):
    aux = lax.axis_index("aux")
    orb = lax.axis_index("orb")
    chip = lax.div(orb, 2)
    core = lax.rem(orb, 2)
    other = 1 - core
    mate = (aux, 2 * chip + other)

    def wrap(at, n):
        return jnp.where(at >= n, at - n, jnp.where(at < 0, at + n, at))

    def ring(shift):
        return wrap(chip + shift, chips)

    def remote(src, dst, snd, rcv, to):
        return pltpu.make_async_remote_copy(
            src_ref=src, dst_ref=dst, send_sem=snd, recv_sem=rcv, device_id=to, device_id_type=MESH
        )

    load_t = pltpu.make_async_copy(t_hbm, tbuf, t_sem)
    load_t.start()

    barrier = pltpu.get_barrier_semaphore()

    def greet(to):
        pl.semaphore_signal(barrier, inc=1, device_id=to, device_id_type=MESH)

    rings = [ring(i) for i in range(-REACH, REACH + 1)]

    def along(act):
        act(ring(chips // 2))

        @pl.loop(1, chips // 2)
        def _(i):
            act(ring(chips // 2 - i))
            act(ring(i - chips // 2))

    def across(act):
        @pl.loop(1, aux_n)
        def _(i):
            act(wrap(aux + i, aux_n))

    def greet_chip(z):
        for c in range(2):
            greet((aux, 2 * z + c))

    along(greet_chip)
    greet(mate)
    across(lambda a: greet((a, orb)))

    row = lax.broadcasted_iota(jnp.int32, (256, 256), 0)
    col = lax.broadcasted_iota(jnp.int32, (256, 256), 1)
    perm[...] = jnp.where(row == lax.rem(col, 16) * 16 + lax.div(col, 16), 1.0, 0.0).astype(BF16)

    dens = dens_ref[...].astype(F32)
    d_rot[0:4, :] = dens[:, :LANES]
    d_rot[4:8, :] = dens[:, :LANES]
    d_rot[8:12, :] = dens[:, LANES:]
    d_rot[12:16, :] = dens[:, LANES:]
    mine = lax.div(lax.broadcasted_iota(jnp.int32, (8, LANES), 0), 4) == core
    left, right = (jnp.where(mine, d_rot[8 * b : 8 * b + 8, :], 0.0) for b in range(2))
    took = lax.broadcasted_iota(jnp.int32, (LANES, LANES), 0)
    gives = lax.broadcasted_iota(jnp.int32, (LANES, LANES), 1)
    for c in range(2):
        want = lax.div(gives, 8) * 16 + 8 * c + lax.rem(gives, 8)
        d_out[c] = jnp.dot(left, jnp.where(took == want, 1.0, 0.0), preferred_element_type=F32) + jnp.dot(
            right, jnp.where(took + LANES == want, 1.0, 0.0), preferred_element_type=F32
        )
    d_in[2 * chip + core] = d_out[core]
    line = lax.broadcasted_iota(jnp.int32, (8, LANES), 0)
    nu_out[...] = jnp.where(line == 0, nu_ref[0, 0], jnp.where(line == 1, nu_ref[0, 1], nu_ref[0, 2]))
    for n in range(2 * aux_n):
        pair_of[n] = n // 2

    virt = virt_ref[...].astype(F32)
    for b in range(4):
        piece[pl.ds(b, 4, stride=4), :] = virt[:, b * LANES : (b + 1) * LANES]
    v_all[core, aux, chip] = piece[...].astype(BF16)

    load_t.wait()

    @pl.loop(0, 3 * BLK // 8)
    def _(i):
        rows = tbuf[lax.div(i, 8), pl.ds(lax.rem(i, 8) * 8, 8)]
        big[pl.ds(pl.multiple_of(i * 512, 512), 512), :] = rows.astype(F32).reshape(512, LANES)

    @pl.loop(0, BLK)
    def _(m):
        tt[core, m] = big[pl.ds(m, 3 * BLK, stride=BLK), :].astype(BF16)

    pl.semaphore_wait(barrier, (2 * chips - 1) + (aux_n - 1))

    def d_sent(z, c):
        at = d_in.at[2 * chip + core]
        return remote(d_out.at[c], at, a_snd.at[2 * z + c], a_rcv.at[2 * chip + core], (aux, 2 * z + c))

    def d_came(z, c):
        return remote(d_out.at[0], d_in.at[2 * z + c], a_snd.at[0], a_rcv.at[2 * z + c], mate)

    def both_cores(act):
        def on_chip(z):
            for c in range(2):
                act(z, c)

        along(on_chip)
        act(chip, other)

    both_cores(lambda z, c: d_sent(z, c).start())

    t_mate = remote(tt.at[core], tt.at[core], m_snd.at[0], m_rcv.at[0], mate)
    nu_copy = remote(nu_out, nu_in, m_snd.at[1], m_rcv.at[1], mate)
    nu_copy.start()
    t_mate.start()

    both_cores(lambda z, c: d_came(z, c).wait_recv())

    rows = (lambda two: two[:, 0] + two[:, 1])(d_in[...].reshape(chips, 2, 8, LANES)).reshape(2 * BLK, LANES).T
    for b in range(2):
        d_rot[b * LANES : (b + 1) * LANES, :] = rows
    first = pl.multiple_of(8 * ring(REACH + 1), 8)
    turned_d = d_rot[pl.ds(first, LANES), :].astype(BF16)
    d_parts = (d_first, d_second)
    for h in range(2):
        d_parts[h][aux] = turned_d[h * BLK : (h + 1) * BLK]

    def d_over(h, a):
        mine_d = d_parts[h].at[aux]
        return remote(mine_d, mine_d, b_snd.at[h, a], b_rcv.at[h, aux], (a, orb))

    def d_from(h, a):
        theirs = d_parts[h].at[a]
        return remote(theirs, theirs, b_snd.at[h, a], b_rcv.at[h, a], (a, orb))

    across(lambda a: d_over(0, a).start())

    def v_sent(z):
        mine_v = v_all.at[core, aux, chip]
        return remote(mine_v, mine_v, e_snd.at[z], e_rcv.at[chip], (aux, 2 * z + core))

    def v_came(z):
        theirs = v_all.at[core, aux, z]
        return remote(theirs, theirs, e_snd.at[z], e_rcv.at[z], mate)

    along(lambda z: v_sent(z).start())

    def v_over(a):
        mine_v = v_all.at[core, aux]
        return remote(mine_v, mine_v, w_snd.at[a], w_rcv.at[aux], (a, orb))

    def v_from(a):
        theirs = v_all.at[core, a]
        return remote(theirs, theirs, w_snd.at[a], w_rcv.at[a], (a, orb))

    v_mate = remote(v_all.at[core], v_all.at[core], m_snd.at[2], m_rcv.at[2], mate)

    nu_copy.wait_recv()
    nu_local = pltpu.make_async_copy(nu_in, nu_mate, n_sem)
    nu_local.start()
    nu_local.wait()
    t_mate.wait_recv()

    def choose(h):
        across(lambda a: d_from(h, a).wait_recv())
        spot = lax.div(lax.broadcasted_iota(jnp.int32, (BLK, BLK), 0), 8) + (8 * h + REACH + 1 + chip)
        group = lax.div(lax.rem(spot, chips), 4)
        for n in range(2):
            for s in range(3):
                nu = jnp.where(core == n, nu_ref[0, s], nu_mate[s, 0])
                at = pair_of[nu]
                both = d_parts[h][at].astype(F32)
                rows = jnp.where(nu == 2 * at, both[:, :BLK], both[:, BLK:])
                keep = jnp.where(group < 2, jnp.where(group == 0, pat_ref[0, nu], pat_ref[1, nu]),
                                 jnp.where(group == 2, pat_ref[2, nu], pat_ref[3, nu])) > 0
                d_t[h, n, :, s * BLK : (s + 1) * BLK] = jnp.where(keep, rows, 0.0).astype(BF16)

    def halves(h, order, ready):
        @pl.loop(0, BLK // 2, unroll=4)
        def _(i):
            for n in range(2):
                two = jnp.concatenate([tt[n, 2 * i], tt[n, 2 * i + 1]], axis=1)
                prod = jnp.dot(d_t[h, n, :, : 3 * BLK], two, preferred_element_type=F32).astype(BF16)
                mid[n * BLK + 2 * i] = prod[:, :LANES]
                mid[n * BLK + 2 * i + 1] = prod[:, LANES:]

        for g in order:
            cols = slice(g * 16, g * 16 + 16)
            for i in range(0, 8, 2):
                two = [mid[16 * n : 16 * n + 16, cols, :].reshape(256, LANES) for n in (i, i + 1)]
                prod = jnp.dot(perm[...], jnp.concatenate(two, axis=1), preferred_element_type=F32).astype(BF16)
                for n in range(2):
                    val = prod[:, n * LANES : (n + 1) * LANES].reshape(2, 8, 16, LANES)
                    x[8 * h + 2 * g : 8 * h + 2 * g + 2, :, 16 * (i + n) : 16 * (i + n) + 16, :] = val
            ready(g)

    def spot_of(e):
        return (e - REACH - 1) % chips

    def far_copy(way, j, q):
        sign = 1 - 2 * way
        cols = pl.ds(q * PAIR, PAIR)
        src = x.at[spot_of(sign * (REACH + j)), cols]
        dst = far.at[way, min(j, REACH - 1) - 1, cols]
        if j == REACH:
            src = x.at[spot_of(sign * (REACH + j)), cols, pl.ds(way * BLK, BLK)]
            dst = far_end.at[way, cols]
        return remote(src, dst, f_snd.at[way, j - 1, q], f_rcv.at[way, j - 1, q], (aux, 2 * rings[REACH + sign * j] + core))

    def send_far(g):
        for way in range(2):
            for j in range(REACH, 0, -1):
                if spot_of((1 - 2 * way) * (REACH + j)) // 2 == g:
                    pl.loop(0, CHUNKS)(lambda q: far_copy(way, j, q).start())

    choose(0)
    halves(0, (1, 0, 2, 3), send_far)

    across(lambda a: d_over(1, a).start())
    along(lambda z: v_came(z).wait_recv())
    across(lambda a: v_over(a).start())

    choose(1)
    halves(1, range(4), lambda g: None)

    across(lambda a: v_from(a).wait_recv())
    v_mate.start()
    v_mate.wait_recv()

    v_blocks = v_all.reshape(2, 2 * aux_n, chips // 2, 16, LANES)

    def turned(first, second, put):
        for n, o in enumerate((first, second)):
            b = bm_ref[o]
            for c in range(2):
                v_sc[n, :, c] = v_blocks[c, b].astype(F32)
        flat = v_sc.reshape(2 * 4 * BLK, LANES)
        for b in range(4):
            rows = flat[pl.ds(b, 2 * BLK, stride=4), :]
            put(slice(b * LANES, (b + 1) * LANES), rows.T.astype(BF16))

    def put_own(rows, val):
        v_own[rows, :] = val
        for way in range(2):
            v_far[way, rows, 0:LANES] = val

    turned(2 * chip, 2 * chip + 1, put_own)
    for way in range(2):
        for j in range(1, REACH + 1):
            z = rings[REACH + (-j if way == 0 else j)]

            def put_far(rows, val):
                v_far[way, rows, j * LANES : (j + 1) * LANES] = val

            if j < REACH:
                turned(2 * z, 2 * z + 1, put_far)
            else:
                turned(2 * z + way, 2 * z + way, put_far)

    both_cores(lambda z, c: d_sent(z, c).wait_send())
    along(lambda z: v_sent(z).wait_send())
    for h in range(2):
        across(lambda a: d_over(h, a).wait_send())
    across(lambda a: v_over(a).wait_send())
    t_mate.wait_send()
    nu_copy.wait_send()
    v_mate.wait_send()

    def hop_copy(way, k, q):
        sign = 1 - 2 * way
        src = part.at[way, q] if k == 0 else hop.at[way, k - 1, q]
        return remote(src, hop.at[way, k, q], p_snd.at[way, k, q], p_rcv.at[way, k, q], (aux, 2 * rings[REACH + sign] + core))

    depth = (2 * REACH + 1) * BLK

    @pl.loop(0, CHUNKS)
    def _(q):
        for way in range(2):
            for j in range(1, REACH + 1):
                far_copy(way, j, q).wait_recv()
            cols = []
            for k in range(PAIR):
                lam = q * PAIR + k
                blocks = [x[spot_of((1 - 2 * way) * REACH), lam]]
                blocks += [far[way, j, lam] for j in range(REACH - 1)] + [far_end[way, lam]]
                cols.append(jnp.concatenate(blocks, axis=0))
            terms = jnp.concatenate(cols, axis=1)
            part[way, q] = jnp.dot(v_far[way, :, :depth], terms, preferred_element_type=F32).astype(BF16)
            hop_copy(way, 0, q).start()

    def own_term(e, q):
        terms = jnp.concatenate([x[spot_of(e), q * PAIR + k] for k in range(PAIR)], axis=1)
        return jnp.dot(v_own[...], terms, preferred_element_type=F32)

    for k in range(REACH - 1):
        @pl.loop(0, CHUNKS)
        def _(q):
            for way in range(2):
                hop_copy(way, k, q).wait_recv()
                e = (1 - 2 * way) * (REACH - 1 - k)
                total = own_term(e, q) + hop[way, k, q].astype(F32)
                hop[way, k, q] = total.astype(BF16)
                hop_copy(way, k + 1, q).start()
                hop_copy(way, k, q).wait_send()
                if k == 0:
                    for j in range(1, REACH + 1):
                        far_copy(way, j, q).wait_send()

    @pl.loop(0, CHUNKS)
    def _(q):
        total = own_term(0, q)
        for way in range(2):
            hop_copy(way, REACH - 1, q).wait_recv()
            total += hop[way, REACH - 1, q].astype(F32)
            hop_copy(way, REACH - 1, q).wait_send()
        for k in range(PAIR):
            big[pl.ds(q * PAIR + k, 512, stride=8), :] = total[:, k * LANES : (k + 1) * LANES]

    @pl.loop(0, 16, unroll=4)
    def _(i):
        rows = pl.ds(pl.multiple_of(i * 256, 256), 256)
        out_ref[rows, :] = big[rows, :].astype(BF16)


def on_device(tensor, nu_index, density, density_pattern, blockmap, virtual):
    aux_n, orb_n = lax.axis_size("aux"), lax.axis_size("orb")
    chips = orb_n // 2
    dma = pltpu.SemaphoreType.DMA
    vmem = pl.BlockSpec(memory_space=pltpu.VMEM)
    smem = pl.BlockSpec(memory_space=pltpu.SMEM)
    out = pl.pallas_call(
        functools.partial(kernel, aux_n, chips),
        out_shape=jax.ShapeDtypeStruct((512 * 8, LANES), BF16),
        in_specs=[smem, smem, smem, vmem, vmem, pl.BlockSpec(memory_space=pl.ANY)],
        out_specs=vmem,
        scratch_shapes=[
            pltpu.VMEM((3, BLK, BLK, LANES), BF16),
            pltpu.VMEM((3 * BLK * BLK, LANES), F32),
            pltpu.VMEM((2, BLK, 3 * BLK, LANES), BF16),
            pltpu.VMEM((16, LANES), F32),
            pltpu.VMEM((8, LANES), jnp.int32),
            pltpu.VMEM((8, LANES), jnp.int32),
            pltpu.SMEM((8, LANES), jnp.int32),
            pltpu.SMEM((2 * aux_n,), jnp.int32),
            pltpu.VMEM((2, 8, LANES), F32),
            pltpu.VMEM((2 * chips, 8, LANES), F32),
            pltpu.VMEM((2 * LANES, LANES), F32),
            pltpu.VMEM((aux_n, BLK, LANES), BF16),
            pltpu.VMEM((aux_n, BLK, LANES), BF16),
            pltpu.VMEM((2, 2, BLK, 4 * BLK), BF16),
            pltpu.VMEM((2, aux_n, chips, 16, LANES), BF16),
            pltpu.VMEM((2, 8, 2, 16, LANES), F32),
            pltpu.VMEM((512, LANES), BF16),
            pltpu.VMEM((2, 512, (REACH + 1) * LANES), BF16),
            pltpu.VMEM((256, 256), BF16),
            pltpu.VMEM((2 * BLK, BLK, LANES), BF16),
            pltpu.VMEM((chips, 8, 2 * BLK, LANES), BF16),
            pltpu.VMEM((2, REACH - 1, 8, 2 * BLK, LANES), BF16),
            pltpu.VMEM((2, 8, BLK, LANES), BF16),
            pltpu.VMEM((2, CHUNKS, 512, PAIR * LANES), BF16),
            pltpu.VMEM((2, REACH, CHUNKS, 512, PAIR * LANES), BF16),
            dma, dma,
            dma((2 * chips,)), dma((2 * chips,)),
            dma((chips,)), dma((chips,)),
            dma((2, aux_n)), dma((2, aux_n)),
            dma((aux_n,)), dma((aux_n,)),
            dma((3,)), dma((3,)),
            dma((2, REACH, CHUNKS)), dma((2, REACH, CHUNKS)),
            dma((2, REACH, CHUNKS)), dma((2, REACH, CHUNKS)),
        ],
        compiler_params=pltpu.CompilerParams(
            collective_id=0, has_side_effects=True, vmem_limit_bytes=56 * 2**20
        ),
        cost_estimate=pl.CostEstimate(flops=3 * 10**9, bytes_accessed=5 * 2**20, transcendentals=0),
        name="contract",
    )(nu_index, density_pattern.T, blockmap, density, virtual, tensor)
    return out.reshape(512, 8, LANES)


def solution(mesh):
    in_specs = (
        P("orb", None, None, "aux"),
        P("orb", None),
        P(("aux", "orb"), None),
        P(),
        P(),
        P(("aux", "orb"), None),
    )
    out_specs = P(None, "orb", "aux")
    return jax.shard_map(
        on_device, mesh=mesh, in_specs=in_specs, out_specs=out_specs, check_vma=False
    )
```
